32 devices in a mesh: groups: 2 (over x), row: 16 (over z, y, core).
Axes of the slice: x: 2, y: 2, z: 4, core: 2. Of those that a mesh axis runs over, the one named last changes fastest.
Arguments:
- enc_dict: bfloat16 [8192, 4096], P('row'), may hold values from -0.09375 to 0.09375
- dec_dict: bfloat16 [8192, 4096], P('row'), may hold values from -0.09375 to 0.09375
- active_ids: int32 [4096], P(('groups', 'row')), parts along dimension 0, may hold values from 0 to 8191, as said below
- counts: int32 [32], P(('groups', 'row')), parts along dimension 0, may hold values from 1 to 128
- strengths: float32 [4096], P(('groups', 'row')), parts along dimension 0, may hold values from 0.25 to 4
- layers: int32 [4096], P(('groups', 'row')), parts along dimension 0, may hold values from 0 to 25
- positions: int32 [4096], P(('groups', 'row')), parts along dimension 0, may hold values from 0 to 127
- targets: float32 [4096, 128], P(('groups', 'row')), parts along dimension 0, may hold values from -6 to 6
Outputs:
- influence: float32 [4096, 128], P(('groups', 'row')), parts along dimension 0
The draws below stay inside these ranges and needn't reach their ends.
There are 2 independent parts, one for each index of `groups`. The reference program is written for one: setup_inputs(seed, part) draws one part's arguments, and reference() takes and returns one part's arrays. A program takes and returns all parts, laid end to end along the dimension named above; an argument that names none is the same for every part. Nothing has to cross between parts.
Inputs may be any that keep to these rules, and one draw needn't show every extreme that they name: `active_ids`: the ids in the d-th block of 128 slots are distinct, increasing, and lie in d * 512 to (d + 1) * 512 - 1.
All inputs are finite; a program needn't handle non-finite values.
Results may differ from the reference program's by a relative error of at most 0.0029.
Values may be sent and summed in bfloat16 or wider, within the bound.
A program may use at most 128 MiB of HBM per device.

```python
import math
import jax
import jax.numpy as jnp
from jax import lax

D = 4096
ROW_FEATURES = 512
ROW_SLOT_LIMIT = 128
TARGET_COUNT = 128
LAYER_COUNT = 26
TOKEN_POSITIONS = 128
NF = 8192
ACTIVE_SLOTS = 2048


def draw_active_ids(key, part):
    key = jax.random.fold_in(key, 11)
    owner_rows = NF // ROW_FEATURES
    row_index = jnp.arange(ROW_FEATURES, dtype=jnp.int32)
    influence_scores = jax.random.randint(key, (owner_rows, ROW_FEATURES), 0, 16384) * ROW_FEATURES + row_index[None, :]
    extra_credit = jnp.where((row_index == 0) | (row_index == ROW_FEATURES - 1), 16384 * ROW_FEATURES, 0)
    chosen_features = lax.top_k(influence_scores + extra_credit[None, :], ROW_SLOT_LIMIT)[1]
    ordered = jnp.sort(chosen_features, axis=1)
    base = jnp.arange(owner_rows, dtype=jnp.int32)[:, None] * ROW_FEATURES
    return (ordered + base).reshape(-1).astype(jnp.int32)


def draw_counts(key, part):
    key = jax.random.fold_in(key, 12)
    owner_rows = ACTIVE_SLOTS // ROW_SLOT_LIMIT
    first, second, third = jax.random.split(key, 3)
    activation_values = jax.random.randint(first, (owner_rows,), 1, ROW_SLOT_LIMIT + 1)
    top_at = jax.random.randint(second, (), 0, owner_rows)
    low_at = (top_at + 1 + jax.random.randint(third, (), 0, owner_rows - 1)) % owner_rows
    activation_values = activation_values.at[top_at].set(ROW_SLOT_LIMIT)
    activation_values = activation_values.at[low_at].set(1)
    return activation_values.astype(jnp.int32)


def draw_positions(key, part):
    key = jax.random.fold_in(key, 13)
    slot_number = jnp.arange(ACTIVE_SLOTS, dtype=jnp.int32)
    spread_amount = jax.random.randint(key, (ACTIVE_SLOTS,), 0, TOKEN_POSITIONS)
    activation_values = (spread_amount + slot_number * TOKEN_POSITIONS // ACTIVE_SLOTS) // 2
    activation_values = activation_values.at[0].set(0)
    activation_values = activation_values.at[ACTIVE_SLOTS - 1].set(TOKEN_POSITIONS - 1)
    return activation_values.astype(jnp.int32)


def touch_ends(entries, stream_key, low, high):
    shape = entries.shape
    place = [jax.random.randint(jax.random.fold_in(stream_key, axis), (), 0, shape[axis]) for axis in range(len(shape))]
    entries = entries.at[tuple(place)].set(low)
    longest = shape.index(max(shape))
    place[longest] = (place[longest] + 1) % shape[longest]
    return entries.at[tuple(place)].set(high)


def levels(rng, shape, cuts, smallest, largest):
    def one(position, shards_of):
        draws = jax.random.uniform(jax.random.fold_in(jax.random.fold_in(rng, 6), position), (shards_of,), jnp.float32, smallest / len(cuts), largest / len(cuts))
        return jnp.repeat(jnp.exp(draws), shape[position] // shards_of).reshape((-1,) + (1,) * (len(shape) - position - 1))

    gain = one(*cuts[0])
    for cut in cuts[1:]:
        gain = gain * one(*cut)
    return gain


def scatter_about(stream_key, dims, deviation, bound, shards=(), kind=jnp.bfloat16):
    array = deviation * jax.random.normal(stream_key, dims, jnp.float32)
    if shards:
        array = array * levels(stream_key, dims, shards, -0.22, 0.18)
    return jnp.clip(array, -bound, bound).astype(kind)


def setup_inputs(seed: int = 0, part: int = 0) -> dict:
    arg_keys = jax.random.split(jax.random.key(seed), 9)
    own_keys = jax.random.split(jax.random.fold_in(arg_keys[8], part), 9)
    enc_dict = scatter_about(arg_keys[0], (NF, D), D ** -0.5, 0.09375, ((0, 16),))
    dec_dict = scatter_about(arg_keys[1], (NF, D), D ** -0.5, 0.09375, ((0, 16),))
    active_ids = draw_active_ids(jax.random.fold_in(jax.random.fold_in(arg_keys[8], part), 71), part)
    counts = draw_counts(jax.random.fold_in(jax.random.fold_in(arg_keys[8], part), 71), part)
    strengths = jnp.clip(jnp.exp(math.log(4.0) - 2.7725887 * jax.random.uniform(own_keys[4], (ACTIVE_SLOTS,), jnp.float32) ** levels(own_keys[4], (ACTIVE_SLOTS,), ((0, 16),), -0.2, 0.2)), 0.25, 4.0)
    layers = touch_ends(jax.random.randint(own_keys[5], (ACTIVE_SLOTS,), 0, LAYER_COUNT), jax.random.fold_in(own_keys[5], 1), 0, LAYER_COUNT - 1).astype(jnp.int32)
    positions = draw_positions(jax.random.fold_in(jax.random.fold_in(arg_keys[8], part), 71), part)
    targets = scatter_about(own_keys[7], (ACTIVE_SLOTS, TARGET_COUNT), 1.0, 6.0, ((0, 16),), jnp.float32)
    return {"enc_dict": enc_dict, "dec_dict": dec_dict, "active_ids": active_ids, "counts": counts, "strengths": strengths, "layers": layers, "positions": positions, "targets": targets}


FLOOR = 1.0


def reference(enc_dict, dec_dict, active_ids, counts, strengths, layers, positions, targets):
    slot_number = jnp.arange(ACTIVE_SLOTS, dtype=jnp.int32)
    live = (slot_number % ROW_SLOT_LIMIT) < counts[slot_number // ROW_SLOT_LIMIT]
    weight = jnp.where(live, strengths, jnp.float32(0.0))
    sources = (weight[:, None] * dec_dict[active_ids].astype(jnp.float32)).astype(jnp.bfloat16)
    receivers = jnp.where(live[:, None], enc_dict[active_ids], jnp.zeros((), jnp.bfloat16))

    def edge_block(block):
        rows, row_layer, row_pos = block
        prod = lax.dot_general(rows, receivers, (((1,), (1,)), ((), ())), preferred_element_type=jnp.float32)
        keep = (row_layer[:, None] < layers[None, :]) & (row_pos[:, None] <= positions[None, :])
        return jnp.where(keep, prod, jnp.float32(0.0))

    edge_weights = lax.map(edge_block, (sources.reshape(-1, ROW_SLOT_LIMIT, D), layers.reshape(-1, ROW_SLOT_LIMIT), positions.reshape(-1, ROW_SLOT_LIMIT)))
    edge_weights = edge_weights.reshape(ACTIVE_SLOTS, ACTIVE_SLOTS)
    inverse = 1.0 / jnp.maximum(jnp.sum(jnp.abs(edge_weights), axis=0), jnp.float32(FLOOR))
    state = targets
    total = jnp.zeros_like(targets)
    for step in range(3):
        state = jnp.dot(edge_weights, inverse[:, None] * state, precision=lax.Precision.HIGHEST, preferred_element_type=jnp.float32)
        total = total + state
    return total
```

```python
import functools

import jax
import jax.numpy as jnp
from jax import lax
from jax.experimental import pallas as pl
from jax.experimental.pallas import tpu as pltpu
from jax.sharding import PartitionSpec as P

FLOOR = 1.0


def swapped(array, axis, stride):
    return lax.ppermute(array, axis, [(i, i ^ 1 << stride) for i in range(lax.axis_size(axis))])


def arrange(mine, other, bit, row_index):
    upper = row_index >> bit & 1 == 1
    return jnp.where(upper, jnp.concatenate([other, mine], 0), jnp.concatenate([mine, other], 0))


def split_half(activation_values, bit, row_index):
    upper = row_index >> bit & 1 == 1
    size = activation_values.shape[0] // 2
    lower_part = activation_values[:size]
    upper_part = activation_values[size:]
    keep = jnp.where(upper, upper_part, lower_part)
    send = jnp.where(upper, lower_part, upper_part)
    return (keep, send)


def members(bit_list, row_index):
    mask = 0
    for bit in bit_list:
        mask = mask | 1 << bit
    spots = jnp.arange(1 << len(bit_list), dtype=jnp.int32)
    devices = jnp.zeros_like(spots) + (row_index & ~mask)
    for order, bit in enumerate(bit_list):
        devices = devices | (spots >> order & 1) << bit
    return devices


def gather_sources(activation_values, bit_list, row_index):
    for bit in bit_list:
        activation_values = arrange(
            activation_values, swapped(activation_values, "row", bit), bit, row_index
        )
    return activation_values


def gather_receivers(activation_values, bit_list, row_index):
    for bit in bit_list:
        activation_values = arrange(
            activation_values, swapped(activation_values, "row", bit), bit, row_index
        )
    return activation_values


def gather_power(activation_values, bit_list, row_index):
    for bit in bit_list:
        activation_values = arrange(
            activation_values, swapped(activation_values, "row", bit), bit, row_index
        )
    return activation_values


def reduce_power(activation_values, bit_list, row_index):
    for bit in reversed(bit_list):
        keep, send = split_half(activation_values, bit, row_index)
        activation_values = keep + swapped(send, "row", bit)
    return activation_values


def per_device(enc_dict, dec_dict, active_ids, counts, strengths, layers, positions, targets):
    bits = lax.axis_size("row").bit_length() - 1
    half = bits // 2
    row_index = lax.axis_index("row")
    row_bits = list(range(half))
    col_bits = list(range(half, bits))
    feat_local = enc_dict.shape[0]
    slots = active_ids.shape[0]
    local = active_ids - row_index * feat_local
    live = jnp.arange(slots, dtype=jnp.int32) < counts[0]
    weight = jnp.where(live, strengths, jnp.float32(0.0))
    sources = (weight[:, None] * dec_dict[local].astype(jnp.float32)).astype(jnp.bfloat16)
    receivers = jnp.where(live[:, None], enc_dict[local], jnp.zeros((), jnp.bfloat16))
    all_layers, all_positions = (
        lax.all_gather(layers, "row", axis=0, tiled=True),
        lax.all_gather(positions, "row", axis=0, tiled=True),
    )
    all_layers = all_layers.reshape(-1, slots)
    all_positions = all_positions.reshape(-1, slots)
    row_devices = members(row_bits, row_index)
    col_devices = members(col_bits, row_index)
    row_layer = all_layers[row_devices].reshape(-1)
    row_pos = all_positions[row_devices].reshape(-1)
    col_layer = all_layers[col_devices].reshape(-1)
    col_pos = all_positions[col_devices].reshape(-1)
    source_block = gather_sources(sources, row_bits, row_index)
    receiver_block = gather_receivers(receivers, col_bits, row_index)
    edge_weights = lax.dot_general(
        source_block, receiver_block, (((1,), (1,)), ((), ())), preferred_element_type=jnp.float32
    )
    keep = (row_layer[:, None] < col_layer[None, :]) & (row_pos[:, None] <= col_pos[None, :])
    edge_weights = jnp.where(keep, edge_weights, jnp.float32(0.0))
    magnitude = jnp.sum(jnp.abs(edge_weights), axis=0)
    for bit in col_bits:
        magnitude = magnitude + swapped(magnitude, "row", bit)
    edge_weights = edge_weights * (1.0 / jnp.maximum(magnitude, jnp.float32(FLOOR)))[None, :]
    own_scale = jnp.ones((slots,), jnp.float32)
    state = targets
    total = jnp.zeros_like(targets)
    for step in range(3):
        inputs = gather_power(own_scale[:, None] * state, col_bits, row_index)
        partial_rows = jnp.dot(
            edge_weights,
            inputs,
            precision=lax.Precision.HIGHEST,
            preferred_element_type=jnp.float32,
        )
        state = reduce_power(partial_rows, row_bits, row_index)
        total = total + state
    return total


MESH = pl.DeviceIdType.MESH
CHUNKS = 8
F32 = jnp.float32
WIRE = jnp.bfloat16


def line_kernel(
    ids_ref, strength_ref, layer_ref, position_ref, count_ref, target_ref, enc_ref, dec_ref,
    out_ref,
    encv, decv, sel, weight, s_buf, r_buf, acc, meta, tbuf, xf, part, total, rs_out, rs_in,
    x_out, x_in, mag, mag_in, res,
    enc_sem, dec_sem, s_recv, s_send, c_send, r_recv, r_send, meta_recv, meta_send,
    t_recv, t_send, mag_sem, rs_send, rs_recv, x_send, x_recv, res_sem,
):
    slots = ids_ref.shape[1]
    feats = enc_ref.shape[0]
    width = enc_ref.shape[1] // CHUNKS
    me = lax.axis_index("row")
    z, yc = me // 4, me % 4
    y, c = yc // 2, yc % 2
    half = z // 2
    is_mid = (z == 1) | (z == 2)
    inner = jnp.where(is_mid, 1, 0)
    mid_z, end_z = 1 + half, 3 * half
    mid_id = mid_z * 4 + yc
    end_id = end_z * 4 + yc
    other_mid = (2 - half) * 4 + yc
    y_peer = z * 4 + (1 - y) * 2 + c
    c_peer = z * 4 + y * 2 + 1 - c
    r_dst = jnp.where(is_mid, other_mid, mid_id)
    s_dst = jnp.where(is_mid, y_peer, mid_id)
    q_own = half * 2 + inner
    q_end = half * 2
    b_own = yc * 2 + inner
    b_end = yc * 2
    ny = (1 - y) * 2 + c

    def s_copy(k, b, dst, send):
        rows = pl.ds(pl.multiple_of(b * slots, slots), slots)
        return pltpu.make_async_remote_copy(
            src_ref=s_buf.at[k, rows], dst_ref=s_buf.at[k, rows], send_sem=send.at[k, b],
            recv_sem=s_recv.at[k, b], device_id={"row": dst}, device_id_type=MESH,
        )

    def r_copy(k, q, dst):
        rows = pl.ds(pl.multiple_of(q * slots, slots), slots)
        return pltpu.make_async_remote_copy(
            src_ref=r_buf.at[k, rows], dst_ref=r_buf.at[k, rows], send_sem=r_send.at[k, q],
            recv_sem=r_recv.at[k, q], device_id={"row": dst}, device_id_type=MESH,
        )

    def meta_copy(slot, which, dst):
        return pltpu.make_async_remote_copy(
            src_ref=meta.at[slot], dst_ref=meta.at[slot], send_sem=meta_send.at[which],
            recv_sem=meta_recv.at[slot], device_id={"row": dst}, device_id_type=MESH,
        )

    def t_copy(q, which, dst):
        rows = pl.ds(pl.multiple_of(q * slots, slots), slots)
        return pltpu.make_async_remote_copy(
            src_ref=tbuf.at[rows], dst_ref=tbuf.at[rows], send_sem=t_send.at[which],
            recv_sem=t_recv.at[q], device_id={"row": dst}, device_id_type=MESH,
        )

    def enc_load(k):
        cols = pl.ds(pl.multiple_of(k * width, width), width)
        return pltpu.make_async_copy(enc_ref.at[:, cols], encv.at[k], enc_sem.at[k])

    def dec_load(k):
        cols = pl.ds(pl.multiple_of(k * width, width), width)
        return pltpu.make_async_copy(dec_ref.at[:, cols], decv.at[k], dec_sem.at[k])

    for k in range(CHUNKS):
        enc_load(k).start()
        dec_load(k).start()

    barrier = pltpu.get_barrier_semaphore()
    for step in range(1, 16):
        pl.semaphore_signal(
            barrier, inc=1, device_id={"row": lax.rem(me + step, 16)}, device_id_type=MESH
        )

    live = lax.broadcasted_iota(jnp.int32, (1, slots), 1) < count_ref[0]
    local = jnp.where(live, ids_ref[...] - me * feats, -1)
    for tile in range(feats // slots):
        feature = lax.broadcasted_iota(jnp.int32, (slots, slots), 0) + tile * slots
        hot = jnp.where(feature == local, 1.0, 0.0).astype(F32)
        sel[:, tile * slots:(tile + 1) * slots] = hot.T.astype(jnp.bfloat16)
    row = jnp.where(live, strength_ref[...], 0.0)
    weight[...] = jnp.broadcast_to(row, (slots, slots)).T

    rows8 = lax.broadcasted_iota(jnp.int32, (8, slots), 0)
    meta[me] = jnp.where(
        rows8 == 0,
        jnp.broadcast_to(layer_ref[...], (8, slots)),
        jnp.broadcast_to(position_ref[...], (8, slots)),
    ).astype(F32)
    tbuf[pl.ds(pl.multiple_of(q_own * slots, slots), slots), :] = target_ref[...]

    pl.semaphore_wait(barrier, 15)

    def produce(k, carry):
        enc_load(k).wait()
        picked = jnp.dot(sel[...], encv[k], preferred_element_type=F32)
        r_buf[k, pl.ds(pl.multiple_of(q_own * slots, slots), slots), :] = picked.astype(
            jnp.bfloat16
        )
        r_copy(k, q_own, r_dst).start()
        dec_load(k).wait()
        picked = jnp.dot(sel[...], decv[k], preferred_element_type=F32) * weight[:, :1]
        s_buf[k, pl.ds(pl.multiple_of(b_own * slots, slots), slots), :] = picked.astype(
            jnp.bfloat16
        )
        s_copy(k, b_own, s_dst, s_send).start()

        @pl.when(is_mid)
        def _():
            s_copy(k, b_own, c_peer, c_send).start()

        return carry

    lax.fori_loop(0, 2, produce, 0)
    for which in range(8):
        @pl.when(me != 4 + which)
        def _():
            meta_copy(me, which, 4 + which).start()
    for which in range(2):
        @pl.when(z != 1 + which)
        def _():
            t_copy(q_own, which, (1 + which) * 4 + yc).start()
    lax.fori_loop(2, CHUNKS, produce, 0)

    @pl.when(is_mid)
    def _():
        acc[...] = jnp.zeros_like(acc)

        def forward(k):
            r_copy(k, q_end, other_mid).wait_recv()
            r_copy(k, q_end, other_mid).start()
            s_copy(k, b_end, y_peer, s_send).wait_recv()
            s_copy(k, b_end, y_peer, s_send).start()
            s_copy(k, b_end, c_peer, c_send).start()
            s_copy(k, ny * 2 + 1, c_peer, c_send).wait_recv()
            s_copy(k, ny * 2 + 1, c_peer, c_send).start()

        def across(k):
            s_copy(k, ny * 2, c_peer, c_send).wait_recv()
            s_copy(k, ny * 2, c_peer, c_send).start()

        def multiply(k):
            for yy in range(2):
                for zl in range(2):
                    s_copy(k, (yy * 2 + 1 - c) * 2 + zl, c_peer, c_send).wait_recv()
            for zl in range(2):
                r_copy(k, (1 - half) * 2 + zl, other_mid).wait_recv()

            def tile(i, carry):
                rows = pl.ds(pl.multiple_of(i * 256, 256), 256)
                acc[rows, :] += lax.dot_general(
                    s_buf[k, rows, :], r_buf[k], (((1,), (1,)), ((), ())),
                    preferred_element_type=F32,
                )
                return carry

            lax.fori_loop(0, acc.shape[0] // 256, tile, 0)

        def first(k, carry):
            forward(k)
            return carry

        lax.fori_loop(0, CHUNKS // 2, first, 0)

        def second(k, carry):
            forward(k)
            j = 2 * (k - CHUNKS // 2)

            @pl.when(j > 0)
            def _():
                multiply(j - 2)
                multiply(j - 1)

            across(j)
            across(j + 1)
            return carry

        lax.fori_loop(CHUNKS // 2, CHUNKS, second, 0)

        for z_from in range(4):
            for d in range(4):
                slot = z_from * 4 + d

                @pl.when(me != slot)
                def _():
                    meta_copy(slot, 0, me).wait_recv()
        for q in range(4):
            @pl.when(q_own != q)
            def _():
                t_copy(q, 0, me).wait_recv()

        def last(k, carry):
            multiply(k)
            return carry

        lax.fori_loop(CHUNKS - 2, CHUNKS, last, 0)

        mag[...] = jnp.zeros_like(mag)

        def mask_rows(b, carry):
            row_z = jnp.where(b % 2 == 1, mid_z, end_z)
            info = meta[row_z * 4 + b // 2]
            row_layer = jnp.broadcast_to(info[0:1], (slots, slots)).T
            row_pos = jnp.broadcast_to(info[1:2], (slots, slots)).T
            rows = pl.ds(pl.multiple_of(b * slots, slots), slots)
            for q, col_z in enumerate((0, 1, 3, 2)):
                other = meta[col_z * 4 + yc]
                keep = (row_layer < other[0:1]) & (row_pos <= other[1:2])
                cols = slice(q * slots, (q + 1) * slots)
                kept = jnp.where(keep, acc[rows, cols], 0.0)
                acc[rows, cols] = kept
                mag[0:1, cols] += jnp.sum(jnp.abs(kept), axis=0, keepdims=True)
            return carry

        lax.fori_loop(0, 8, mask_rows, 0)
        mag_copy = pltpu.make_async_remote_copy(
            src_ref=mag, dst_ref=mag_in, send_sem=mag_sem.at[0], recv_sem=mag_sem.at[1],
            device_id={"row": other_mid}, device_id_type=MESH,
        )
        mag_copy.start()
        mag_copy.wait()
        inverse = 1.0 / jnp.maximum(mag[0:1, :] + mag_in[0:1, :], FLOOR)

        def scale(i, carry):
            rows = pl.ds(pl.multiple_of(i * 64, 64), 64)
            acc[rows, :] = acc[rows, :] * inverse
            return carry

        lax.fori_loop(0, acc.shape[0] // 64, scale, 0)
        xf[...] = tbuf[...]
        total[...] = jnp.zeros_like(total)

        def rs_copy(t, slot, d, dst):
            return pltpu.make_async_remote_copy(
                src_ref=rs_out.at[t, d], dst_ref=rs_in.at[t, slot], send_sem=rs_send.at[t, d],
                recv_sem=rs_recv.at[t, slot], device_id={"row": dst}, device_id_type=MESH,
            )

        def x_copy(t):
            return pltpu.make_async_remote_copy(
                src_ref=x_out.at[t], dst_ref=x_in.at[t], send_sem=x_send.at[t],
                recv_sem=x_recv.at[t], device_id={"row": other_mid}, device_id_type=MESH,
            )

        def power(t, carry):
            def product(d):
                rows = pl.ds(pl.multiple_of(d * 2 * slots, 2 * slots), 2 * slots)
                return jnp.dot(
                    acc[rows, :], xf[...], precision=lax.Precision.HIGHEST,
                    preferred_element_type=F32,
                )

            def send_part(i, carry):
                d = jnp.where(i == 0, ny, jnp.where(i == 1, (1 - y) * 2 + 1 - c, y * 2 + 1 - c))
                rs_out[t, d] = product(d).astype(WIRE)
                rs_copy(t, yc, d, z * 4 + d).start()
                return carry

            lax.fori_loop(0, 3, send_part, 0)
            part[...] = product(yc)
            for d in (ny, (1 - y) * 2 + 1 - c, y * 2 + 1 - c):
                rs_copy(t, d, d, z * 4 + d).wait_recv()
                part[...] += rs_in[t, d].astype(F32)
            total[...] += part[...]

            @pl.when(t < 2)
            def _():
                x_out[t] = part[...].astype(WIRE)
                x_copy(t).start()
                mine = pl.ds(pl.multiple_of(half * 2 * slots, 2 * slots), 2 * slots)
                theirs = pl.ds(pl.multiple_of((1 - half) * 2 * slots, 2 * slots), 2 * slots)
                xf[mine, :] = part[...]
                x_copy(t).wait_recv()
                xf[theirs, :] = x_in[t].astype(F32)

            return carry

        lax.fori_loop(0, 3, power, 0)

    res_copy = pltpu.make_async_remote_copy(
        src_ref=total.at[pl.ds(0, slots)], dst_ref=res, send_sem=res_sem.at[0],
        recv_sem=res_sem.at[1], device_id={"row": jnp.where(is_mid, end_id, mid_id)},
        device_id_type=MESH,
    )

    @pl.when(is_mid)
    def _():
        res_copy.start()
        out_ref[...] = total[slots:2 * slots, :]

        def drain(k, carry):
            r_copy(k, q_end, other_mid).wait_send()
            s_copy(k, b_end, y_peer, s_send).wait_send()
            for b in (b_own, b_end, ny * 2, ny * 2 + 1):
                s_copy(k, b, c_peer, c_send).wait_send()
            return carry

        lax.fori_loop(0, CHUNKS, drain, 0)

        def drain_power(t, carry):
            for d in (ny, (1 - y) * 2 + 1 - c, y * 2 + 1 - c):
                pltpu.make_async_remote_copy(
                    src_ref=rs_out.at[t, d], dst_ref=rs_in.at[t, d], send_sem=rs_send.at[t, d],
                    recv_sem=rs_recv.at[t, d], device_id={"row": z * 4 + d}, device_id_type=MESH,
                ).wait_send()
            return carry

        lax.fori_loop(0, 3, drain_power, 0)
        for t in range(2):
            pltpu.make_async_remote_copy(
                src_ref=x_out.at[t], dst_ref=x_in.at[t], send_sem=x_send.at[t],
                recv_sem=x_recv.at[t], device_id={"row": other_mid}, device_id_type=MESH,
            ).wait_send()
        res_copy.wait_send()

    def drain_own(k, carry):
        r_copy(k, q_own, r_dst).wait_send()
        s_copy(k, b_own, s_dst, s_send).wait_send()
        return carry

    lax.fori_loop(0, CHUNKS, drain_own, 0)
    for which in range(8):
        @pl.when(me != 4 + which)
        def _():
            meta_copy(me, which, 4 + which).wait_send()
    for which in range(2):
        @pl.when(z != 1 + which)
        def _():
            t_copy(q_own, which, (1 + which) * 4 + yc).wait_send()

    @pl.when(jnp.logical_not(is_mid))
    def _():
        res_copy.wait_recv()
        out_ref[...] = res[...]


def per_device_line(enc_dict, dec_dict, active_ids, counts, strengths, layers, positions, targets):
    slots = active_ids.shape[0]
    feats, depth = enc_dict.shape
    width = depth // CHUNKS
    outs = targets.shape[1]
    vmem = pl.BlockSpec(memory_space=pltpu.VMEM)
    dma = pltpu.SemaphoreType.DMA
    bf16 = jnp.bfloat16
    return pl.pallas_call(
        line_kernel,
        out_shape=jax.ShapeDtypeStruct(targets.shape, F32),
        in_specs=[vmem] * 4
        + [pl.BlockSpec(memory_space=pltpu.SMEM), vmem]
        + [pl.BlockSpec(memory_space=pl.ANY)] * 2,
        out_specs=vmem,
        scratch_shapes=[
            pltpu.VMEM((CHUNKS, feats, width), bf16),
            pltpu.VMEM((CHUNKS, feats, width), bf16),
            pltpu.VMEM((slots, feats), bf16),
            pltpu.VMEM((slots, slots), F32),
            pltpu.VMEM((CHUNKS, 8 * slots, width), bf16),
            pltpu.VMEM((CHUNKS, 4 * slots, width), bf16),
            pltpu.VMEM((8 * slots, 4 * slots), F32),
            pltpu.VMEM((16, 8, slots), F32),
            pltpu.VMEM((4 * slots, outs), F32),
            pltpu.VMEM((4 * slots, outs), F32),
            pltpu.VMEM((2 * slots, outs), F32),
            pltpu.VMEM((2 * slots, outs), F32),
            pltpu.VMEM((3, 4, 2 * slots, outs), WIRE),
            pltpu.VMEM((3, 4, 2 * slots, outs), WIRE),
            pltpu.VMEM((2, 2 * slots, outs), WIRE),
            pltpu.VMEM((2, 2 * slots, outs), WIRE),
            pltpu.VMEM((8, 4 * slots), F32),
            pltpu.VMEM((8, 4 * slots), F32),
            pltpu.VMEM((slots, outs), F32),
            dma((CHUNKS,)),
            dma((CHUNKS,)),
            dma((CHUNKS, 8)),
            dma((CHUNKS, 8)),
            dma((CHUNKS, 8)),
            dma((CHUNKS, 4)),
            dma((CHUNKS, 4)),
            dma((16,)),
            dma((8,)),
            dma((4,)),
            dma((2,)),
            dma((2,)),
            dma((3, 4)),
            dma((3, 4)),
            dma((2,)),
            dma((2,)),
            dma((2,)),
        ],
        compiler_params=pltpu.CompilerParams(
            collective_id=0, has_side_effects=True, vmem_limit_bytes=48 * 1024 * 1024
        ),
    )(
        active_ids.reshape(1, slots),
        strengths.reshape(1, slots),
        layers.reshape(1, slots),
        positions.reshape(1, slots),
        counts,
        targets,
        enc_dict,
        dec_dict,
    )


def solution(mesh):
    in_specs = (
        P("row", None),
        P("row", None),
        P(("groups", "row")),
        P(("groups", "row")),
        P(("groups", "row")),
        P(("groups", "row")),
        P(("groups", "row")),
        P(("groups", "row"), None),
    )
    out_specs = P(("groups", "row"), None)
    return jax.shard_map(
        per_device_line if mesh.shape["row"] == 16 else per_device,
        mesh=mesh,
        in_specs=in_specs,
        out_specs=out_specs,
        check_vma=False,
    )
```

```python
import functools

import jax
import jax.numpy as jnp
from jax import lax
from jax.experimental import pallas as pl
from jax.experimental.pallas import tpu as pltpu
from jax.sharding import PartitionSpec as P

FLOOR = 1.0


def swapped(array, axis, stride):
    return lax.ppermute(array, axis, [(i, i ^ 1 << stride) for i in range(lax.axis_size(axis))])


def arrange(mine, other, bit, row_index):
    upper = row_index >> bit & 1 == 1
    return jnp.where(upper, jnp.concatenate([other, mine], 0), jnp.concatenate([mine, other], 0))


def split_half(activation_values, bit, row_index):
    upper = row_index >> bit & 1 == 1
    size = activation_values.shape[0] // 2
    lower_part = activation_values[:size]
    upper_part = activation_values[size:]
    keep = jnp.where(upper, upper_part, lower_part)
    send = jnp.where(upper, lower_part, upper_part)
    return (keep, send)


def members(bit_list, row_index):
    mask = 0
    for bit in bit_list:
        mask = mask | 1 << bit
    spots = jnp.arange(1 << len(bit_list), dtype=jnp.int32)
    devices = jnp.zeros_like(spots) + (row_index & ~mask)
    for order, bit in enumerate(bit_list):
        devices = devices | (spots >> order & 1) << bit
    return devices


def gather_sources(activation_values, bit_list, row_index):
    for bit in bit_list:
        activation_values = arrange(
            activation_values, swapped(activation_values, "row", bit), bit, row_index
        )
    return activation_values


def gather_receivers(activation_values, bit_list, row_index):
    for bit in bit_list:
        activation_values = arrange(
            activation_values, swapped(activation_values, "row", bit), bit, row_index
        )
    return activation_values


def gather_power(activation_values, bit_list, row_index):
    for bit in bit_list:
        activation_values = arrange(
            activation_values, swapped(activation_values, "row", bit), bit, row_index
        )
    return activation_values


def reduce_power(activation_values, bit_list, row_index):
    for bit in reversed(bit_list):
        keep, send = split_half(activation_values, bit, row_index)
        activation_values = keep + swapped(send, "row", bit)
    return activation_values


def per_device(enc_dict, dec_dict, active_ids, counts, strengths, layers, positions, targets):
    bits = lax.axis_size("row").bit_length() - 1
    half = bits // 2
    row_index = lax.axis_index("row")
    row_bits = list(range(half))
    col_bits = list(range(half, bits))
    feat_local = enc_dict.shape[0]
    slots = active_ids.shape[0]
    local = active_ids - row_index * feat_local
    live = jnp.arange(slots, dtype=jnp.int32) < counts[0]
    weight = jnp.where(live, strengths, jnp.float32(0.0))
    sources = (weight[:, None] * dec_dict[local].astype(jnp.float32)).astype(jnp.bfloat16)
    receivers = jnp.where(live[:, None], enc_dict[local], jnp.zeros((), jnp.bfloat16))
    all_layers, all_positions = (
        lax.all_gather(layers, "row", axis=0, tiled=True),
        lax.all_gather(positions, "row", axis=0, tiled=True),
    )
    all_layers = all_layers.reshape(-1, slots)
    all_positions = all_positions.reshape(-1, slots)
    row_devices = members(row_bits, row_index)
    col_devices = members(col_bits, row_index)
    row_layer = all_layers[row_devices].reshape(-1)
    row_pos = all_positions[row_devices].reshape(-1)
    col_layer = all_layers[col_devices].reshape(-1)
    col_pos = all_positions[col_devices].reshape(-1)
    source_block = gather_sources(sources, row_bits, row_index)
    receiver_block = gather_receivers(receivers, col_bits, row_index)
    edge_weights = lax.dot_general(
        source_block, receiver_block, (((1,), (1,)), ((), ())), preferred_element_type=jnp.float32
    )
    keep = (row_layer[:, None] < col_layer[None, :]) & (row_pos[:, None] <= col_pos[None, :])
    edge_weights = jnp.where(keep, edge_weights, jnp.float32(0.0))
    magnitude = jnp.sum(jnp.abs(edge_weights), axis=0)
    for bit in col_bits:
        magnitude = magnitude + swapped(magnitude, "row", bit)
    edge_weights = edge_weights * (1.0 / jnp.maximum(magnitude, jnp.float32(FLOOR)))[None, :]
    own_scale = jnp.ones((slots,), jnp.float32)
    state = targets
    total = jnp.zeros_like(targets)
    for step in range(3):
        inputs = gather_power(own_scale[:, None] * state, col_bits, row_index)
        partial_rows = jnp.dot(
            edge_weights,
            inputs,
            precision=lax.Precision.HIGHEST,
            preferred_element_type=jnp.float32,
        )
        state = reduce_power(partial_rows, row_bits, row_index)
        total = total + state
    return total


MESH = pl.DeviceIdType.MESH
CHUNKS = 8
F32 = jnp.float32
WIRE = jnp.bfloat16


def line_kernel(
    ids_hbm, strength_hbm, layer_hbm, position_hbm, count_ref, target_hbm, enc_ref, dec_ref,
    out_ref,
    ids_ref, strength_ref, layer_ref, position_ref, encv, decv, sel, weight, s_buf, r_buf, acc, meta, tbuf, xf, part, total, rs_out, rs_in,
    x_out, x_in, mag, mag_in, res, a_hi, a_lo, x_two,
    small_sem, enc_sem, dec_sem, s_recv, s_send, c_send, r_recv, r_send, meta_recv, meta_send,
    t_recv, t_send, mag_sem, rs_send, rs_recv, x_send, x_recv, res_sem,
):
    slots = ids_hbm.shape[1]
    feats = enc_ref.shape[0]
    width = enc_ref.shape[1] // CHUNKS
    me = lax.axis_index("row")
    z, yc = me // 4, me % 4
    y, c = yc // 2, yc % 2
    half = z // 2
    is_mid = (z == 1) | (z == 2)
    inner = jnp.where(is_mid, 1, 0)
    mid_z, end_z = 1 + half, 3 * half
    mid_id = mid_z * 4 + yc
    end_id = end_z * 4 + yc
    other_mid = (2 - half) * 4 + yc
    y_peer = z * 4 + (1 - y) * 2 + c
    c_peer = z * 4 + y * 2 + 1 - c
    r_dst = jnp.where(is_mid, other_mid, mid_id)
    s_dst = jnp.where(is_mid, y_peer, mid_id)
    q_own = half * 2 + inner
    q_end = half * 2
    b_own = yc * 2 + inner
    b_end = yc * 2
    ny = (1 - y) * 2 + c

    def s_copy(k, b, dst, send):
        rows = pl.ds(pl.multiple_of(b * slots, slots), slots)
        return pltpu.make_async_remote_copy(
            src_ref=s_buf.at[k, rows], dst_ref=s_buf.at[k, rows], send_sem=send.at[k, b],
            recv_sem=s_recv.at[k, b], device_id={"row": dst}, device_id_type=MESH,
        )

    def r_copy(k, q, dst):
        rows = pl.ds(pl.multiple_of(q * slots, slots), slots)
        return pltpu.make_async_remote_copy(
            src_ref=r_buf.at[k, rows], dst_ref=r_buf.at[k, rows], send_sem=r_send.at[k, q],
            recv_sem=r_recv.at[k, q], device_id={"row": dst}, device_id_type=MESH,
        )

    def meta_copy(slot, which, dst):
        return pltpu.make_async_remote_copy(
            src_ref=meta.at[slot], dst_ref=meta.at[slot], send_sem=meta_send.at[which],
            recv_sem=meta_recv.at[slot], device_id={"row": dst}, device_id_type=MESH,
        )

    def t_copy(q, which, dst):
        rows = pl.ds(pl.multiple_of(q * slots, slots), slots)
        return pltpu.make_async_remote_copy(
            src_ref=tbuf.at[rows], dst_ref=tbuf.at[rows], send_sem=t_send.at[which],
            recv_sem=t_recv.at[q], device_id={"row": dst}, device_id_type=MESH,
        )

    def enc_load(k):
        cols = pl.ds(pl.multiple_of(k * width, width), width)
        return pltpu.make_async_copy(enc_ref.at[:, cols], encv.at[k], enc_sem.at[k])

    def dec_load(k):
        cols = pl.ds(pl.multiple_of(k * width, width), width)
        return pltpu.make_async_copy(dec_ref.at[:, cols], decv.at[k], dec_sem.at[k])

    own = pl.ds(pl.multiple_of(q_own * slots, slots), slots)
    small = [
        pltpu.make_async_copy(source, place, small_sem.at[i])
        for i, (source, place) in enumerate((
            (ids_hbm, ids_ref), (strength_hbm, strength_ref), (layer_hbm, layer_ref),
            (position_hbm, position_ref), (target_hbm, tbuf.at[own]),
        ))
    ]
    for copy in small:
        copy.start()
    for k in range(CHUNKS):
        enc_load(k).start()
        dec_load(k).start()

    barrier = pltpu.get_barrier_semaphore()
    for step in range(1, 16):
        pl.semaphore_signal(
            barrier, inc=1, device_id={"row": lax.rem(me + step, 16)}, device_id_type=MESH
        )

    for copy in small:
        copy.wait()
    live = lax.broadcasted_iota(jnp.int32, (1, slots), 1) < count_ref[0]
    local = jnp.where(live, ids_ref[...] - me * feats, -1)
    for tile in range(feats // slots):
        feature = lax.broadcasted_iota(jnp.int32, (slots, slots), 0) + tile * slots
        hot = jnp.where(feature == local, 1.0, 0.0).astype(F32)
        sel[:, tile * slots:(tile + 1) * slots] = hot.T.astype(jnp.bfloat16)
    row = jnp.where(live, strength_ref[...], 0.0)
    weight[...] = jnp.broadcast_to(row, (slots, slots)).T

    rows8 = lax.broadcasted_iota(jnp.int32, (8, slots), 0)
    meta[me] = jnp.where(
        rows8 == 0,
        jnp.broadcast_to(layer_ref[...], (8, slots)),
        jnp.broadcast_to(position_ref[...], (8, slots)),
    ).astype(F32)

    pl.semaphore_wait(barrier, 15)

    def produce(k, carry):
        enc_load(k).wait()
        picked = jnp.dot(sel[...], encv[k], preferred_element_type=F32)
        r_buf[k, pl.ds(pl.multiple_of(q_own * slots, slots), slots), :] = picked.astype(
            jnp.bfloat16
        )
        r_copy(k, q_own, r_dst).start()
        dec_load(k).wait()
        picked = jnp.dot(sel[...], decv[k], preferred_element_type=F32) * weight[:, :1]
        s_buf[k, pl.ds(pl.multiple_of(b_own * slots, slots), slots), :] = picked.astype(
            jnp.bfloat16
        )
        s_copy(k, b_own, s_dst, s_send).start()

        @pl.when(is_mid)
        def _():
            s_copy(k, b_own, c_peer, c_send).start()

        return carry

    lax.fori_loop(0, 2, produce, 0)
    for which in range(8):
        @pl.when(me != 4 + which)
        def _():
            meta_copy(me, which, 4 + which).start()
    for which in range(2):
        @pl.when(z != 1 + which)
        def _():
            t_copy(q_own, which, (1 + which) * 4 + yc).start()
    lax.fori_loop(2, CHUNKS, produce, 0)

    @pl.when(is_mid)
    def _():
        acc[...] = jnp.zeros_like(acc)

        def forward(k):
            r_copy(k, q_end, other_mid).wait_recv()
            r_copy(k, q_end, other_mid).start()
            s_copy(k, b_end, y_peer, s_send).wait_recv()
            s_copy(k, b_end, y_peer, s_send).start()
            s_copy(k, b_end, c_peer, c_send).start()
            s_copy(k, ny * 2 + 1, c_peer, c_send).wait_recv()
            s_copy(k, ny * 2 + 1, c_peer, c_send).start()

        def across(k):
            s_copy(k, ny * 2, c_peer, c_send).wait_recv()
            s_copy(k, ny * 2, c_peer, c_send).start()

        def multiply(k):
            for yy in range(2):
                for zl in range(2):
                    s_copy(k, (yy * 2 + 1 - c) * 2 + zl, c_peer, c_send).wait_recv()
            for zl in range(2):
                r_copy(k, (1 - half) * 2 + zl, other_mid).wait_recv()

            def tile(i, carry):
                rows = pl.ds(pl.multiple_of(i * 256, 256), 256)
                acc[rows, :] += lax.dot_general(
                    s_buf[k, rows, :], r_buf[k], (((1,), (1,)), ((), ())),
                    preferred_element_type=F32,
                )
                return carry

            lax.fori_loop(0, acc.shape[0] // 256, tile, 0)

        def first(k, carry):
            forward(k)
            return carry

        lax.fori_loop(0, CHUNKS // 2, first, 0)

        def second(k, carry):
            forward(k)
            j = 2 * (k - CHUNKS // 2)

            @pl.when(j > 0)
            def _():
                multiply(j - 2)
                multiply(j - 1)

            across(j)
            across(j + 1)
            return carry

        lax.fori_loop(CHUNKS // 2, CHUNKS, second, 0)

        for z_from in range(4):
            for d in range(4):
                slot = z_from * 4 + d

                @pl.when(me != slot)
                def _():
                    meta_copy(slot, 0, me).wait_recv()
        for q in range(4):
            @pl.when(q_own != q)
            def _():
                t_copy(q, 0, me).wait_recv()

        def last(k, carry):
            multiply(k)
            return carry

        lax.fori_loop(CHUNKS - 2, CHUNKS, last, 0)

        mag[...] = jnp.zeros_like(mag)

        def mask_rows(b, carry):
            row_z = jnp.where(b % 2 == 1, mid_z, end_z)
            info = meta[row_z * 4 + b // 2]
            row_layer = jnp.broadcast_to(info[0:1], (slots, slots)).T
            row_pos = jnp.broadcast_to(info[1:2], (slots, slots)).T
            rows = pl.ds(pl.multiple_of(b * slots, slots), slots)
            for q, col_z in enumerate((0, 1, 3, 2)):
                other = meta[col_z * 4 + yc]
                keep = (row_layer < other[0:1]) & (row_pos <= other[1:2])
                cols = slice(q * slots, (q + 1) * slots)
                kept = jnp.where(keep, acc[rows, cols], 0.0)
                acc[rows, cols] = kept
                mag[0:1, cols] += jnp.sum(jnp.abs(kept), axis=0, keepdims=True)
            return carry

        lax.fori_loop(0, 8, mask_rows, 0)
        mag_copy = pltpu.make_async_remote_copy(
            src_ref=mag, dst_ref=mag_in, send_sem=mag_sem.at[0], recv_sem=mag_sem.at[1],
            device_id={"row": other_mid}, device_id_type=MESH,
        )
        mag_copy.start()
        mag_copy.wait()
        inverse = 1.0 / jnp.maximum(mag[0:1, :] + mag_in[0:1, :], FLOOR)

        def scale(i, carry):
            rows = pl.ds(pl.multiple_of(i * 64, 64), 64)
            scaled = acc[rows, :] * inverse
            high = scaled.astype(jnp.bfloat16)
            a_hi[rows, :] = high
            a_lo[rows, :] = (scaled - high.astype(F32)).astype(jnp.bfloat16)
            return carry

        lax.fori_loop(0, acc.shape[0] // 64, scale, 0)
        xf[...] = tbuf[...]
        total[...] = jnp.zeros_like(total)

        def rs_copy(t, slot, d, dst):
            return pltpu.make_async_remote_copy(
                src_ref=rs_out.at[t, d], dst_ref=rs_in.at[t, slot], send_sem=rs_send.at[t, d],
                recv_sem=rs_recv.at[t, slot], device_id={"row": dst}, device_id_type=MESH,
            )

        def x_copy(t):
            return pltpu.make_async_remote_copy(
                src_ref=x_out.at[t], dst_ref=x_in.at[t], send_sem=x_send.at[t],
                recv_sem=x_recv.at[t], device_id={"row": other_mid}, device_id_type=MESH,
            )

        outs = xf.shape[1]

        def power(t, carry):
            high = xf[...].astype(jnp.bfloat16)
            x_two[:, :outs] = high
            x_two[:, outs:] = (xf[...] - high.astype(F32)).astype(jnp.bfloat16)

            def product(d):
                rows = pl.ds(pl.multiple_of(d * 2 * slots, 2 * slots), 2 * slots)
                two = jnp.dot(a_hi[rows, :], x_two[...], preferred_element_type=F32)
                low = jnp.dot(a_lo[rows, :], x_two[:, :outs], preferred_element_type=F32)
                return two[:, :outs] + (two[:, outs:] + low)

            def send_part(i, carry):
                d = jnp.where(i == 0, ny, jnp.where(i == 1, (1 - y) * 2 + 1 - c, y * 2 + 1 - c))
                rs_out[t, d] = product(d).astype(WIRE)
                rs_copy(t, yc, d, z * 4 + d).start()
                return carry

            lax.fori_loop(0, 3, send_part, 0)
            part[...] = product(yc)
            for d in (ny, (1 - y) * 2 + 1 - c, y * 2 + 1 - c):
                rs_copy(t, d, d, z * 4 + d).wait_recv()
                part[...] += rs_in[t, d].astype(F32)
            total[...] += part[...]

            @pl.when(t < 2)
            def _():
                x_out[t] = part[...].astype(WIRE)
                x_copy(t).start()
                mine = pl.ds(pl.multiple_of(half * 2 * slots, 2 * slots), 2 * slots)
                theirs = pl.ds(pl.multiple_of((1 - half) * 2 * slots, 2 * slots), 2 * slots)
                xf[mine, :] = part[...]
                x_copy(t).wait_recv()
                xf[theirs, :] = x_in[t].astype(F32)

            return carry

        lax.fori_loop(0, 3, power, 0)

    res_copy = pltpu.make_async_remote_copy(
        src_ref=total.at[pl.ds(0, slots)], dst_ref=res, send_sem=res_sem.at[0],
        recv_sem=res_sem.at[1], device_id={"row": jnp.where(is_mid, end_id, mid_id)},
        device_id_type=MESH,
    )

    @pl.when(is_mid)
    def _():
        res_copy.start()
        out_ref[...] = total[slots:2 * slots, :]

        def drain(k, carry):
            r_copy(k, q_end, other_mid).wait_send()
            s_copy(k, b_end, y_peer, s_send).wait_send()
            for b in (b_own, b_end, ny * 2, ny * 2 + 1):
                s_copy(k, b, c_peer, c_send).wait_send()
            return carry

        lax.fori_loop(0, CHUNKS, drain, 0)

        def drain_power(t, carry):
            for d in (ny, (1 - y) * 2 + 1 - c, y * 2 + 1 - c):
                pltpu.make_async_remote_copy(
                    src_ref=rs_out.at[t, d], dst_ref=rs_in.at[t, d], send_sem=rs_send.at[t, d],
                    recv_sem=rs_recv.at[t, d], device_id={"row": z * 4 + d}, device_id_type=MESH,
                ).wait_send()
            return carry

        lax.fori_loop(0, 3, drain_power, 0)
        for t in range(2):
            pltpu.make_async_remote_copy(
                src_ref=x_out.at[t], dst_ref=x_in.at[t], send_sem=x_send.at[t],
                recv_sem=x_recv.at[t], device_id={"row": other_mid}, device_id_type=MESH,
            ).wait_send()
        res_copy.wait_send()

    def drain_own(k, carry):
        r_copy(k, q_own, r_dst).wait_send()
        s_copy(k, b_own, s_dst, s_send).wait_send()
        return carry

    lax.fori_loop(0, CHUNKS, drain_own, 0)
    for which in range(8):
        @pl.when(me != 4 + which)
        def _():
            meta_copy(me, which, 4 + which).wait_send()
    for which in range(2):
        @pl.when(z != 1 + which)
        def _():
            t_copy(q_own, which, (1 + which) * 4 + yc).wait_send()

    @pl.when(jnp.logical_not(is_mid))
    def _():
        res_copy.wait_recv()
        out_ref[...] = res[...]


def per_device_line(enc_dict, dec_dict, active_ids, counts, strengths, layers, positions, targets):
    slots = active_ids.shape[0]
    feats, depth = enc_dict.shape
    width = depth // CHUNKS
    outs = targets.shape[1]
    hbm = pl.BlockSpec(memory_space=pltpu.HBM)
    vmem = pl.BlockSpec(memory_space=pltpu.VMEM)
    dma = pltpu.SemaphoreType.DMA
    bf16 = jnp.bfloat16
    return pl.pallas_call(
        line_kernel,
        out_shape=jax.ShapeDtypeStruct(targets.shape, F32),
        in_specs=[hbm] * 4 + [pl.BlockSpec(memory_space=pltpu.SMEM)] + [hbm] * 3,
        out_specs=vmem,
        scratch_shapes=[
            pltpu.VMEM((1, slots), jnp.int32),
            pltpu.VMEM((1, slots), F32),
            pltpu.VMEM((1, slots), jnp.int32),
            pltpu.VMEM((1, slots), jnp.int32),
            pltpu.VMEM((CHUNKS, feats, width), bf16),
            pltpu.VMEM((CHUNKS, feats, width), bf16),
            pltpu.VMEM((slots, feats), bf16),
            pltpu.VMEM((slots, slots), F32),
            pltpu.VMEM((CHUNKS, 8 * slots, width), bf16),
            pltpu.VMEM((CHUNKS, 4 * slots, width), bf16),
            pltpu.VMEM((8 * slots, 4 * slots), F32),
            pltpu.VMEM((16, 8, slots), F32),
            pltpu.VMEM((4 * slots, outs), F32),
            pltpu.VMEM((4 * slots, outs), F32),
            pltpu.VMEM((2 * slots, outs), F32),
            pltpu.VMEM((2 * slots, outs), F32),
            pltpu.VMEM((3, 4, 2 * slots, outs), WIRE),
            pltpu.VMEM((3, 4, 2 * slots, outs), WIRE),
            pltpu.VMEM((2, 2 * slots, outs), WIRE),
            pltpu.VMEM((2, 2 * slots, outs), WIRE),
            pltpu.VMEM((8, 4 * slots), F32),
            pltpu.VMEM((8, 4 * slots), F32),
            pltpu.VMEM((slots, outs), F32),
            pltpu.VMEM((8 * slots, 4 * slots), bf16),
            pltpu.VMEM((8 * slots, 4 * slots), bf16),
            pltpu.VMEM((4 * slots, 2 * outs), bf16),
            dma((5,)),
            dma((CHUNKS,)),
            dma((CHUNKS,)),
            dma((CHUNKS, 8)),
            dma((CHUNKS, 8)),
            dma((CHUNKS, 8)),
            dma((CHUNKS, 4)),
            dma((CHUNKS, 4)),
            dma((16,)),
            dma((8,)),
            dma((4,)),
            dma((2,)),
            dma((2,)),
            dma((3, 4)),
            dma((3, 4)),
            dma((2,)),
            dma((2,)),
            dma((2,)),
        ],
        compiler_params=pltpu.CompilerParams(
            collective_id=0, has_side_effects=True, vmem_limit_bytes=60 * 1024 * 1024
        ),
    )(
        active_ids.reshape(1, slots),
        strengths.reshape(1, slots),
        layers.reshape(1, slots),
        positions.reshape(1, slots),
        counts,
        targets,
        enc_dict,
        dec_dict,
    )


def solution(mesh):
    in_specs = (
        P("row", None),
        P("row", None),
        P(("groups", "row")),
        P(("groups", "row")),
        P(("groups", "row")),
        P(("groups", "row")),
        P(("groups", "row")),
        P(("groups", "row"), None),
    )
    out_specs = P(("groups", "row"), None)
    return jax.shard_map(
        per_device_line if mesh.shape["row"] == 16 else per_device,
        mesh=mesh,
        in_specs=in_specs,
        out_specs=out_specs,
        check_vma=False,
    )
```

```python
import functools

import jax
import jax.numpy as jnp
from jax import lax
from jax.experimental import pallas as pl
from jax.experimental.pallas import tpu as pltpu
from jax.sharding import PartitionSpec as P

FLOOR = 1.0


def swapped(array, axis, stride):
    return lax.ppermute(array, axis, [(i, i ^ 1 << stride) for i in range(lax.axis_size(axis))])


def arrange(mine, other, bit, row_index):
    upper = row_index >> bit & 1 == 1
    return jnp.where(upper, jnp.concatenate([other, mine], 0), jnp.concatenate([mine, other], 0))


def split_half(activation_values, bit, row_index):
    upper = row_index >> bit & 1 == 1
    size = activation_values.shape[0] // 2
    lower_part = activation_values[:size]
    upper_part = activation_values[size:]
    keep = jnp.where(upper, upper_part, lower_part)
    send = jnp.where(upper, lower_part, upper_part)
    return (keep, send)


def members(bit_list, row_index):
    mask = 0
    for bit in bit_list:
        mask = mask | 1 << bit
    spots = jnp.arange(1 << len(bit_list), dtype=jnp.int32)
    devices = jnp.zeros_like(spots) + (row_index & ~mask)
    for order, bit in enumerate(bit_list):
        devices = devices | (spots >> order & 1) << bit
    return devices


def gather_sources(activation_values, bit_list, row_index):
    for bit in bit_list:
        activation_values = arrange(
            activation_values, swapped(activation_values, "row", bit), bit, row_index
        )
    return activation_values


def gather_receivers(activation_values, bit_list, row_index):
    for bit in bit_list:
        activation_values = arrange(
            activation_values, swapped(activation_values, "row", bit), bit, row_index
        )
    return activation_values


def gather_power(activation_values, bit_list, row_index):
    for bit in bit_list:
        activation_values = arrange(
            activation_values, swapped(activation_values, "row", bit), bit, row_index
        )
    return activation_values


def reduce_power(activation_values, bit_list, row_index):
    for bit in reversed(bit_list):
        keep, send = split_half(activation_values, bit, row_index)
        activation_values = keep + swapped(send, "row", bit)
    return activation_values


def per_device(enc_dict, dec_dict, active_ids, counts, strengths, layers, positions, targets):
    bits = lax.axis_size("row").bit_length() - 1
    half = bits // 2
    row_index = lax.axis_index("row")
    row_bits = list(range(half))
    col_bits = list(range(half, bits))
    feat_local = enc_dict.shape[0]
    slots = active_ids.shape[0]
    local = active_ids - row_index * feat_local
    live = jnp.arange(slots, dtype=jnp.int32) < counts[0]
    weight = jnp.where(live, strengths, jnp.float32(0.0))
    sources = (weight[:, None] * dec_dict[local].astype(jnp.float32)).astype(jnp.bfloat16)
    receivers = jnp.where(live[:, None], enc_dict[local], jnp.zeros((), jnp.bfloat16))
    all_layers, all_positions = (
        lax.all_gather(layers, "row", axis=0, tiled=True),
        lax.all_gather(positions, "row", axis=0, tiled=True),
    )
    all_layers = all_layers.reshape(-1, slots)
    all_positions = all_positions.reshape(-1, slots)
    row_devices = members(row_bits, row_index)
    col_devices = members(col_bits, row_index)
    row_layer = all_layers[row_devices].reshape(-1)
    row_pos = all_positions[row_devices].reshape(-1)
    col_layer = all_layers[col_devices].reshape(-1)
    col_pos = all_positions[col_devices].reshape(-1)
    source_block = gather_sources(sources, row_bits, row_index)
    receiver_block = gather_receivers(receivers, col_bits, row_index)
    edge_weights = lax.dot_general(
        source_block, receiver_block, (((1,), (1,)), ((), ())), preferred_element_type=jnp.float32
    )
    keep = (row_layer[:, None] < col_layer[None, :]) & (row_pos[:, None] <= col_pos[None, :])
    edge_weights = jnp.where(keep, edge_weights, jnp.float32(0.0))
    magnitude = jnp.sum(jnp.abs(edge_weights), axis=0)
    for bit in col_bits:
        magnitude = magnitude + swapped(magnitude, "row", bit)
    edge_weights = edge_weights * (1.0 / jnp.maximum(magnitude, jnp.float32(FLOOR)))[None, :]
    own_scale = jnp.ones((slots,), jnp.float32)
    state = targets
    total = jnp.zeros_like(targets)
    for step in range(3):
        inputs = gather_power(own_scale[:, None] * state, col_bits, row_index)
        partial_rows = jnp.dot(
            edge_weights,
            inputs,
            precision=lax.Precision.HIGHEST,
            preferred_element_type=jnp.float32,
        )
        state = reduce_power(partial_rows, row_bits, row_index)
        total = total + state
    return total


MESH = pl.DeviceIdType.MESH
CHUNKS = 8
F32 = jnp.float32
WIRE = jnp.bfloat16


def line_kernel(
    ids_hbm, strength_hbm, layer_hbm, position_hbm, count_ref, target_hbm, enc_ref, dec_ref,
    out_ref,
    ids_ref, strength_ref, layer_ref, position_ref, encv, decv, sel, weight, s_buf, r_buf, acc, meta, tbuf, xf, part, total, rs_out, rs_in,
    x_out, x_in, mag, mag_in, res, a_hi, a_lo, x_two,
    small_sem, enc_sem, dec_sem, s_recv, s_send, c_send, r_recv, r_send, meta_recv, meta_send,
    t_recv, t_send, mag_sem, rs_send, rs_recv, x_send, x_recv, res_sem,
):
    slots = ids_hbm.shape[1]
    feats = enc_ref.shape[0]
    width = enc_ref.shape[1] // CHUNKS
    me = lax.axis_index("row")
    z, yc = me // 4, me % 4
    y, c = yc // 2, yc % 2
    half = z // 2
    is_mid = (z == 1) | (z == 2)
    inner = jnp.where(is_mid, 1, 0)
    mid_z, end_z = 1 + half, 3 * half
    mid_id = mid_z * 4 + yc
    end_id = end_z * 4 + yc
    other_mid = (2 - half) * 4 + yc
    y_peer = z * 4 + (1 - y) * 2 + c
    c_peer = z * 4 + y * 2 + 1 - c
    r_dst = jnp.where(is_mid, other_mid, mid_id)
    s_dst = jnp.where(is_mid, y_peer, mid_id)
    q_own = half * 2 + inner
    q_end = half * 2
    b_own = yc * 2 + inner
    b_end = yc * 2
    ny = (1 - y) * 2 + c

    def s_copy(k, b, dst, send):
        rows = pl.ds(pl.multiple_of(b * slots, slots), slots)
        return pltpu.make_async_remote_copy(
            src_ref=s_buf.at[k, rows], dst_ref=s_buf.at[k, rows], send_sem=send.at[k, b],
            recv_sem=s_recv.at[k, b], device_id={"row": dst}, device_id_type=MESH,
        )

    def r_copy(k, q, dst):
        rows = pl.ds(pl.multiple_of(q * slots, slots), slots)
        return pltpu.make_async_remote_copy(
            src_ref=r_buf.at[k, rows], dst_ref=r_buf.at[k, rows], send_sem=r_send.at[k, q],
            recv_sem=r_recv.at[k, q], device_id={"row": dst}, device_id_type=MESH,
        )

    def meta_copy(slot, which, dst):
        return pltpu.make_async_remote_copy(
            src_ref=meta.at[slot], dst_ref=meta.at[slot], send_sem=meta_send.at[which],
            recv_sem=meta_recv.at[slot], device_id={"row": dst}, device_id_type=MESH,
        )

    def t_copy(q, which, dst):
        rows = pl.ds(pl.multiple_of(q * slots, slots), slots)
        return pltpu.make_async_remote_copy(
            src_ref=tbuf.at[rows], dst_ref=tbuf.at[rows], send_sem=t_send.at[which],
            recv_sem=t_recv.at[q], device_id={"row": dst}, device_id_type=MESH,
        )

    def enc_load(k):
        cols = pl.ds(pl.multiple_of(k * width, width), width)
        return pltpu.make_async_copy(enc_ref.at[:, cols], encv.at[k], enc_sem.at[k])

    def dec_load(k):
        cols = pl.ds(pl.multiple_of(k * width, width), width)
        return pltpu.make_async_copy(dec_ref.at[:, cols], decv.at[k], dec_sem.at[k])

    own = pl.ds(pl.multiple_of(q_own * slots, slots), slots)
    small = [
        pltpu.make_async_copy(source, place, small_sem.at[i])
        for i, (source, place) in enumerate((
            (ids_hbm, ids_ref), (strength_hbm, strength_ref), (layer_hbm, layer_ref),
            (position_hbm, position_ref), (target_hbm, tbuf.at[own]),
        ))
    ]
    for copy in small:
        copy.start()
    for k in range(CHUNKS):
        dec_load(k).start()
        enc_load(k).start()

    barrier = pltpu.get_barrier_semaphore()
    for step in range(1, 16):
        pl.semaphore_signal(
            barrier, inc=1, device_id={"row": lax.rem(me + step, 16)}, device_id_type=MESH
        )

    for copy in small:
        copy.wait()
    live = lax.broadcasted_iota(jnp.int32, (1, slots), 1) < count_ref[0]
    local = jnp.where(live, ids_ref[...] - me * feats, -1)
    for tile in range(feats // slots):
        feature = lax.broadcasted_iota(jnp.int32, (slots, slots), 0) + tile * slots
        hot = jnp.where(feature == local, 1.0, 0.0).astype(F32)
        sel[:, tile * slots:(tile + 1) * slots] = hot.T.astype(jnp.bfloat16)
    row = jnp.where(live, strength_ref[...], 0.0)
    weight[...] = jnp.broadcast_to(row, (slots, slots)).T

    rows8 = lax.broadcasted_iota(jnp.int32, (8, slots), 0)
    meta[me] = jnp.where(
        rows8 == 0,
        jnp.broadcast_to(layer_ref[...], (8, slots)),
        jnp.broadcast_to(position_ref[...], (8, slots)),
    ).astype(F32)

    pl.semaphore_wait(barrier, 15)

    def produce(k, carry):
        dec_load(k).wait()
        picked = jnp.dot(sel[...], decv[k], preferred_element_type=F32) * weight[:, :1]
        s_buf[k, pl.ds(pl.multiple_of(b_own * slots, slots), slots), :] = picked.astype(
            jnp.bfloat16
        )
        s_copy(k, b_own, s_dst, s_send).start()

        enc_load(k).wait()
        picked = jnp.dot(sel[...], encv[k], preferred_element_type=F32)
        r_buf[k, pl.ds(pl.multiple_of(q_own * slots, slots), slots), :] = picked.astype(
            jnp.bfloat16
        )
        r_copy(k, q_own, r_dst).start()
        @pl.when(is_mid)
        def _():
            s_copy(k, b_own, c_peer, c_send).start()

        return carry

    lax.fori_loop(0, 2, produce, 0)
    for which in range(8):
        @pl.when(me != 4 + which)
        def _():
            meta_copy(me, which, 4 + which).start()
    for which in range(2):
        @pl.when(z != 1 + which)
        def _():
            t_copy(q_own, which, (1 + which) * 4 + yc).start()
    lax.fori_loop(2, CHUNKS, produce, 0)

    @pl.when(is_mid)
    def _():
        acc[...] = jnp.zeros_like(acc)

        def forward(k):
            s_copy(k, b_end, y_peer, s_send).wait_recv()
            s_copy(k, b_end, y_peer, s_send).start()
            s_copy(k, b_end, c_peer, c_send).start()
            r_copy(k, q_end, other_mid).wait_recv()
            r_copy(k, q_end, other_mid).start()
            s_copy(k, ny * 2 + 1, c_peer, c_send).wait_recv()
            s_copy(k, ny * 2 + 1, c_peer, c_send).start()

        def across(k):
            s_copy(k, ny * 2, c_peer, c_send).wait_recv()
            s_copy(k, ny * 2, c_peer, c_send).start()

        def multiply(k):
            for yy in range(2):
                for zl in range(2):
                    s_copy(k, (yy * 2 + 1 - c) * 2 + zl, c_peer, c_send).wait_recv()
            for zl in range(2):
                r_copy(k, (1 - half) * 2 + zl, other_mid).wait_recv()

            def tile(i, carry):
                rows = pl.ds(pl.multiple_of(i * 256, 256), 256)
                acc[rows, :] += lax.dot_general(
                    s_buf[k, rows, :], r_buf[k], (((1,), (1,)), ((), ())),
                    preferred_element_type=F32,
                )
                return carry

            lax.fori_loop(0, acc.shape[0] // 256, tile, 0)

        def first(k, carry):
            forward(k)
            return carry

        lax.fori_loop(0, CHUNKS // 2, first, 0)

        def second(k, carry):
            forward(k)
            j = 2 * (k - CHUNKS // 2)

            @pl.when(j > 0)
            def _():
                multiply(j - 2)
                multiply(j - 1)

            across(j)
            across(j + 1)
            return carry

        lax.fori_loop(CHUNKS // 2, CHUNKS, second, 0)

        for z_from in range(4):
            for d in range(4):
                slot = z_from * 4 + d

                @pl.when(me != slot)
                def _():
                    meta_copy(slot, 0, me).wait_recv()
        for q in range(4):
            @pl.when(q_own != q)
            def _():
                t_copy(q, 0, me).wait_recv()

        def last(k, carry):
            multiply(k)
            return carry

        lax.fori_loop(CHUNKS - 2, CHUNKS, last, 0)

        mag[...] = jnp.zeros_like(mag)

        def mask_rows(b, carry):
            row_z = jnp.where(b % 2 == 1, mid_z, end_z)
            info = meta[row_z * 4 + b // 2]
            row_layer = jnp.broadcast_to(info[0:1], (slots, slots)).T
            row_pos = jnp.broadcast_to(info[1:2], (slots, slots)).T
            rows = pl.ds(pl.multiple_of(b * slots, slots), slots)
            for q, col_z in enumerate((0, 1, 3, 2)):
                other = meta[col_z * 4 + yc]
                keep = (row_layer < other[0:1]) & (row_pos <= other[1:2])
                cols = slice(q * slots, (q + 1) * slots)
                kept = jnp.where(keep, acc[rows, cols], 0.0)
                acc[rows, cols] = kept
                mag[0:1, cols] += jnp.sum(jnp.abs(kept), axis=0, keepdims=True)
            return carry

        lax.fori_loop(0, 8, mask_rows, 0)
        mag_copy = pltpu.make_async_remote_copy(
            src_ref=mag, dst_ref=mag_in, send_sem=mag_sem.at[0], recv_sem=mag_sem.at[1],
            device_id={"row": other_mid}, device_id_type=MESH,
        )
        mag_copy.start()
        mag_copy.wait()
        inverse = 1.0 / jnp.maximum(mag[0:1, :] + mag_in[0:1, :], FLOOR)

        def scale(i, carry):
            rows = pl.ds(pl.multiple_of(i * 64, 64), 64)
            scaled = acc[rows, :] * inverse
            high = scaled.astype(jnp.bfloat16)
            a_hi[rows, :] = high
            a_lo[rows, :] = (scaled - high.astype(F32)).astype(jnp.bfloat16)
            return carry

        lax.fori_loop(0, acc.shape[0] // 64, scale, 0)
        xf[...] = tbuf[...]
        total[...] = jnp.zeros_like(total)

        def rs_copy(t, slot, d, dst):
            return pltpu.make_async_remote_copy(
                src_ref=rs_out.at[t, d], dst_ref=rs_in.at[t, slot], send_sem=rs_send.at[t, d],
                recv_sem=rs_recv.at[t, slot], device_id={"row": dst}, device_id_type=MESH,
            )

        def x_copy(t):
            return pltpu.make_async_remote_copy(
                src_ref=x_out.at[t], dst_ref=x_in.at[t], send_sem=x_send.at[t],
                recv_sem=x_recv.at[t], device_id={"row": other_mid}, device_id_type=MESH,
            )

        outs = xf.shape[1]

        def power(t, carry):
            high = xf[...].astype(jnp.bfloat16)
            x_two[:, :outs] = high
            x_two[:, outs:] = (xf[...] - high.astype(F32)).astype(jnp.bfloat16)

            def product(d):
                rows = pl.ds(pl.multiple_of(d * 2 * slots, 2 * slots), 2 * slots)
                two = jnp.dot(a_hi[rows, :], x_two[...], preferred_element_type=F32)
                low = jnp.dot(a_lo[rows, :], x_two[:, :outs], preferred_element_type=F32)
                return two[:, :outs] + (two[:, outs:] + low)

            def send_part(i, carry):
                d = jnp.where(i == 0, ny, jnp.where(i == 1, (1 - y) * 2 + 1 - c, y * 2 + 1 - c))
                rs_out[t, d] = product(d).astype(WIRE)
                rs_copy(t, yc, d, z * 4 + d).start()
                return carry

            lax.fori_loop(0, 3, send_part, 0)
            part[...] = product(yc)
            for d in (ny, (1 - y) * 2 + 1 - c, y * 2 + 1 - c):
                rs_copy(t, d, d, z * 4 + d).wait_recv()
                part[...] += rs_in[t, d].astype(F32)
            total[...] += part[...]

            @pl.when(t < 2)
            def _():
                x_out[t] = part[...].astype(WIRE)
                x_copy(t).start()
                mine = pl.ds(pl.multiple_of(half * 2 * slots, 2 * slots), 2 * slots)
                theirs = pl.ds(pl.multiple_of((1 - half) * 2 * slots, 2 * slots), 2 * slots)
                xf[mine, :] = part[...]
                x_copy(t).wait_recv()
                xf[theirs, :] = x_in[t].astype(F32)

            return carry

        lax.fori_loop(0, 3, power, 0)

    res_copy = pltpu.make_async_remote_copy(
        src_ref=total.at[pl.ds(0, slots)], dst_ref=res, send_sem=res_sem.at[0],
        recv_sem=res_sem.at[1], device_id={"row": jnp.where(is_mid, end_id, mid_id)},
        device_id_type=MESH,
    )

    @pl.when(is_mid)
    def _():
        res_copy.start()
        out_ref[...] = total[slots:2 * slots, :]

        def drain(k, carry):
            r_copy(k, q_end, other_mid).wait_send()
            s_copy(k, b_end, y_peer, s_send).wait_send()
            for b in (b_own, b_end, ny * 2, ny * 2 + 1):
                s_copy(k, b, c_peer, c_send).wait_send()
            return carry

        lax.fori_loop(0, CHUNKS, drain, 0)

        def drain_power(t, carry):
            for d in (ny, (1 - y) * 2 + 1 - c, y * 2 + 1 - c):
                pltpu.make_async_remote_copy(
                    src_ref=rs_out.at[t, d], dst_ref=rs_in.at[t, d], send_sem=rs_send.at[t, d],
                    recv_sem=rs_recv.at[t, d], device_id={"row": z * 4 + d}, device_id_type=MESH,
                ).wait_send()
            return carry

        lax.fori_loop(0, 3, drain_power, 0)
        for t in range(2):
            pltpu.make_async_remote_copy(
                src_ref=x_out.at[t], dst_ref=x_in.at[t], send_sem=x_send.at[t],
                recv_sem=x_recv.at[t], device_id={"row": other_mid}, device_id_type=MESH,
            ).wait_send()
        res_copy.wait_send()

    def drain_own(k, carry):
        r_copy(k, q_own, r_dst).wait_send()
        s_copy(k, b_own, s_dst, s_send).wait_send()
        return carry

    lax.fori_loop(0, CHUNKS, drain_own, 0)
    for which in range(8):
        @pl.when(me != 4 + which)
        def _():
            meta_copy(me, which, 4 + which).wait_send()
    for which in range(2):
        @pl.when(z != 1 + which)
        def _():
            t_copy(q_own, which, (1 + which) * 4 + yc).wait_send()

    @pl.when(jnp.logical_not(is_mid))
    def _():
        res_copy.wait_recv()
        out_ref[...] = res[...]


def per_device_line(enc_dict, dec_dict, active_ids, counts, strengths, layers, positions, targets):
    slots = active_ids.shape[0]
    feats, depth = enc_dict.shape
    width = depth // CHUNKS
    outs = targets.shape[1]
    hbm = pl.BlockSpec(memory_space=pltpu.HBM)
    vmem = pl.BlockSpec(memory_space=pltpu.VMEM)
    dma = pltpu.SemaphoreType.DMA
    bf16 = jnp.bfloat16
    return pl.pallas_call(
        line_kernel,
        out_shape=jax.ShapeDtypeStruct(targets.shape, F32),
        in_specs=[hbm] * 4 + [pl.BlockSpec(memory_space=pltpu.SMEM)] + [hbm] * 3,
        out_specs=vmem,
        scratch_shapes=[
            pltpu.VMEM((1, slots), jnp.int32),
            pltpu.VMEM((1, slots), F32),
            pltpu.VMEM((1, slots), jnp.int32),
            pltpu.VMEM((1, slots), jnp.int32),
            pltpu.VMEM((CHUNKS, feats, width), bf16),
            pltpu.VMEM((CHUNKS, feats, width), bf16),
            pltpu.VMEM((slots, feats), bf16),
            pltpu.VMEM((slots, slots), F32),
            pltpu.VMEM((CHUNKS, 8 * slots, width), bf16),
            pltpu.VMEM((CHUNKS, 4 * slots, width), bf16),
            pltpu.VMEM((8 * slots, 4 * slots), F32),
            pltpu.VMEM((16, 8, slots), F32),
            pltpu.VMEM((4 * slots, outs), F32),
            pltpu.VMEM((4 * slots, outs), F32),
            pltpu.VMEM((2 * slots, outs), F32),
            pltpu.VMEM((2 * slots, outs), F32),
            pltpu.VMEM((3, 4, 2 * slots, outs), WIRE),
            pltpu.VMEM((3, 4, 2 * slots, outs), WIRE),
            pltpu.VMEM((2, 2 * slots, outs), WIRE),
            pltpu.VMEM((2, 2 * slots, outs), WIRE),
            pltpu.VMEM((8, 4 * slots), F32),
            pltpu.VMEM((8, 4 * slots), F32),
            pltpu.VMEM((slots, outs), F32),
            pltpu.VMEM((8 * slots, 4 * slots), bf16),
            pltpu.VMEM((8 * slots, 4 * slots), bf16),
            pltpu.VMEM((4 * slots, 2 * outs), bf16),
            dma((5,)),
            dma((CHUNKS,)),
            dma((CHUNKS,)),
            dma((CHUNKS, 8)),
            dma((CHUNKS, 8)),
            dma((CHUNKS, 8)),
            dma((CHUNKS, 4)),
            dma((CHUNKS, 4)),
            dma((16,)),
            dma((8,)),
            dma((4,)),
            dma((2,)),
            dma((2,)),
            dma((3, 4)),
            dma((3, 4)),
            dma((2,)),
            dma((2,)),
            dma((2,)),
        ],
        compiler_params=pltpu.CompilerParams(
            collective_id=0, has_side_effects=True, vmem_limit_bytes=60 * 1024 * 1024
        ),
    )(
        active_ids.reshape(1, slots),
        strengths.reshape(1, slots),
        layers.reshape(1, slots),
        positions.reshape(1, slots),
        counts,
        targets,
        enc_dict,
        dec_dict,
    )


def solution(mesh):
    in_specs = (
        P("row", None),
        P("row", None),
        P(("groups", "row")),
        P(("groups", "row")),
        P(("groups", "row")),
        P(("groups", "row")),
        P(("groups", "row")),
        P(("groups", "row"), None),
    )
    out_specs = P(("groups", "row"), None)
    return jax.shard_map(
        per_device_line if mesh.shape["row"] == 16 else per_device,
        mesh=mesh,
        in_specs=in_specs,
        out_specs=out_specs,
        check_vma=False,
    )
```
